128 devices in a mesh: tile: 32 (over x, z_lo, y), mode: 4 (over z_hi, core).
Axes of the slice: x: 4, y: 4, z: 4 (z_hi: 2, z_lo: 2; z = z_hi * 2 + z_lo), core: 2. Of those that a mesh axis runs over, the one named last changes fastest.
Arguments:
- object_phase: float32 [2, 8192, 512], P(None, 'tile'), may hold values from -3.140625 to 3.140625
- object_absorb: float32 [2, 8192, 512], P(None, 'tile'), may hold values from 0 to 0.5
- probe_modes: float32 [8, 2, 256, 256], P('mode'), may hold values from -6 to 6
- measured: float32 [64, 256, 256], P('tile'), may hold values from 0.5 to 50
- offsets: int32 [64, 2], P('tile'), may hold values from 0 to 256, as said below
- counts: int32 [32], P('tile'), may hold values from 1 to 2, as said below
Outputs:
- grad_phase: float32 [2, 8192, 512], P(None, 'tile', 'mode')
- grad_absorb: float32 [2, 8192, 512], P(None, 'tile', 'mode')
- grad_probe: float32 [8, 2, 256, 256], P('mode')
The draws below stay inside these ranges and needn't reach their ends.
Inputs may be any that keep to these rules, and one draw needn't show every extreme that they name: offsets[p, 0] is below 256 and offsets[p, 1] at most 256, so each patch lies inside its strip's columns and reaches at most 255 rows into the next strip. The first counts[t] slots of tile t are in use, the others are not.
All inputs are finite; a program needn't handle non-finite values.
Results may differ from the reference program's by a relative error of at most 0.0003.
Values sent between devices are 32-bit elements; how exact they have to be, the bound alone decides.
No kernel may reach another device: no remote copies, remote signals or barrier semaphores. Data moves between devices by JAX's collectives and lax.ppermute only.
A program may use at most 128 MiB of HBM per device.

```python
import math
import jax
import jax.numpy as jnp
from jax import lax

PATCH = 256
MODES = 8
SLICES = 2
STRIP = 256
COLUMNS = 512
SLOTS = 2
TILES = 32
ROWS = 8192
POSITIONS = 64


def draw_offsets(key, part):
    key = jax.random.fold_in(key, 11)
    row_key, column_key = jax.random.split(key)
    row_offsets = jax.random.randint(row_key, (POSITIONS, 1), 0, STRIP, dtype=jnp.int32)
    column_offsets = jax.random.randint(column_key, (POSITIONS, 1), 0, COLUMNS - PATCH + 1, dtype=jnp.int32)
    row_offsets = row_offsets.at[1, 0].set(STRIP - 1)
    column_offsets = column_offsets.at[0, 0].set(COLUMNS - PATCH)
    return jnp.concatenate([row_offsets, column_offsets], axis=1)


def draw_counts(key, part):
    key = jax.random.fold_in(key, 23)
    count_key, pick_key = jax.random.split(key)
    loads = jax.random.randint(count_key, (TILES,), 1, SLOTS + 1, dtype=jnp.int32)
    busiest = jax.random.randint(pick_key, (), 0, TILES, dtype=jnp.int32)
    return loads.at[busiest].set(SLOTS)


def levels(rng, shape, pieces, low, largest):
    level = 1.0
    for dim, shards_of in pieces:
        draws = jax.random.uniform(jax.random.fold_in(jax.random.fold_in(rng, 6), dim), (shards_of,), jnp.float32, low / len(pieces), largest / len(pieces))
        level = level * jnp.repeat(jnp.exp(draws), shape[dim] // shards_of).reshape((-1,) + (1,) * (len(shape) - 1 - dim))
    return level


def centred(stream_key, extent, spread, reach, cuts=(), kind=jnp.bfloat16):
    array = spread * jax.random.normal(stream_key, extent, jnp.float32)
    if cuts:
        array = array * levels(stream_key, extent, cuts, -0.22, 0.18)
    return jnp.clip(array, -reach, reach).astype(kind)


def setup_inputs(seed: int = 0) -> dict:
    seeds = jax.random.split(jax.random.key(seed), 7)
    object_phase = jnp.clip(jax.random.uniform(seeds[0], (SLICES, ROWS, COLUMNS), jnp.float32, -3.140625, 3.140625), -3.140625, 3.140625)
    object_absorb = jnp.clip(0.5 * jax.random.uniform(seeds[1], (SLICES, ROWS, COLUMNS), jnp.float32) ** levels(seeds[1], (SLICES, ROWS, COLUMNS), ((1, 32),), -0.2, 0.2), 0.0, 0.5)
    probe_modes = centred(seeds[2], (MODES, 2, PATCH, PATCH), 1.0, 6.0, ((0, 4),), jnp.float32)
    measured = jnp.clip(jnp.exp(math.log(50.0) - 4.6051702 * jax.random.uniform(seeds[3], (POSITIONS, PATCH, PATCH), jnp.float32) ** levels(seeds[3], (POSITIONS, PATCH, PATCH), ((0, 32),), -0.2, 0.2)), 0.5, 50.0)
    offsets = draw_offsets(jax.random.fold_in(seeds[6], 71), 0)
    counts = draw_counts(jax.random.fold_in(seeds[6], 71), 0)
    return {"object_phase": object_phase, "object_absorb": object_absorb, "probe_modes": probe_modes, "measured": measured, "offsets": offsets, "counts": counts}


fresnel_number = 40.0

def propagator(length):
    counter = jnp.arange(length, dtype=jnp.int32)
    freq = ((counter + length // 2) % length - length // 2).astype(jnp.float32) / length
    radial = freq[:, None] ** 2 + freq[None, :] ** 2
    angle_map = -math.pi * fresnel_number * radial
    return (jnp.cos(angle_map), jnp.sin(angle_map))

def far_field(patch_phase, patch_absorb, probe_modes):
    kernel_real, kernel_imag = propagator(PATCH)
    kernel = lax.complex(kernel_real, kernel_imag)
    transmit = jnp.exp(-patch_absorb) * lax.complex(jnp.cos(patch_phase), jnp.sin(patch_phase))
    wave = lax.complex(probe_modes[:, 0], probe_modes[:, 1]) * transmit[0]
    for layer in range(1, SLICES):
        wave = jnp.fft.ifft2(jnp.fft.fft2(wave, norm='ortho') * kernel, norm='ortho') * transmit[layer]
    return jnp.fft.fft2(wave, norm='ortho')

def position_loss(patch_phase, patch_absorb, probe_modes, measured_one, valid):
    field = far_field(patch_phase, patch_absorb, probe_modes)
    intensity = lax.optimization_barrier(jnp.sum(jnp.real(field) ** 2 + jnp.imag(field) ** 2, axis=0))
    misfit = jnp.sqrt(intensity + 1.0) - jnp.sqrt(measured_one + 1.0)
    return 0.5 * valid * jnp.sum(misfit * misfit)

def reference(object_phase, object_absorb, probe_modes, measured, offsets, counts):
    padding = jnp.zeros((SLICES, PATCH, COLUMNS), object_phase.dtype)
    phase_padded = jnp.concatenate([object_phase, padding], axis=1)
    absorb_padded = jnp.concatenate([object_absorb, padding], axis=1)
    patch_shape = (SLICES, PATCH, PATCH)

    def visit(carry, position):
        grad_phase, grad_absorb, grad_probe = carry
        tile_index = position // SLOTS
        valid = (position % SLOTS < counts[tile_index]).astype(object_phase.dtype)
        row_start = (tile_index * STRIP + offsets[position, 0]).astype(jnp.int32)
        column_start = offsets[position, 1].astype(jnp.int32)
        corner = (jnp.int32(0), row_start, column_start)
        patch_phase = lax.dynamic_slice(phase_padded, corner, patch_shape)
        patch_absorb = lax.dynamic_slice(absorb_padded, corner, patch_shape)
        measured_one = measured[position]

        def local_loss(first, second, third):
            return position_loss(first, second, third, measured_one, valid)
        loss_value, pullback = jax.vjp(local_loss, patch_phase, patch_absorb, probe_modes)
        d_phase, d_absorb, d_probe = pullback(jnp.ones_like(loss_value))
        grad_phase = lax.dynamic_update_slice(grad_phase, lax.dynamic_slice(grad_phase, corner, patch_shape) + d_phase, corner)
        grad_absorb = lax.dynamic_update_slice(grad_absorb, lax.dynamic_slice(grad_absorb, corner, patch_shape) + d_absorb, corner)
        return ((grad_phase, grad_absorb, grad_probe + d_probe), None)
    start_state = (jnp.zeros_like(phase_padded), jnp.zeros_like(absorb_padded), jnp.zeros_like(probe_modes))
    final_state, unused = lax.scan(visit, start_state, jnp.arange(POSITIONS, dtype=jnp.int32))
    grad_phase, grad_absorb, grad_probe = final_state
    return (grad_phase[:, :ROWS], grad_absorb[:, :ROWS], grad_probe)
```

```python
import functools
import math

import jax
import jax.numpy as jnp
import ml_dtypes
import numpy as np
from jax import lax
from jax.experimental import pallas as pl
from jax.experimental.pallas import tpu as pltpu
from jax.sharding import PartitionSpec as P

fresnel_number = 40.0
LENGTH = 256
HALF = LENGTH // 2
SLOTS = 2
LOCAL_MODES = 2
TILES = 32
F32 = jnp.float32
BF16 = jnp.bfloat16


def split_table(matrix):
    high = matrix.astype(ml_dtypes.bfloat16)
    low = (matrix - high.astype(np.float64)).astype(ml_dtypes.bfloat16)
    return high, low


@functools.lru_cache(maxsize=None)
def constant_tables():
    counter = np.arange(LENGTH)
    angle = 2.0 * np.pi / LENGTH * ((counter[:, None] * counter[None, :]) % LENGTH)
    dft = np.exp(-1j * angle) / math.sqrt(LENGTH)
    freq = ((counter + HALF) % LENGTH - HALF) / LENGTH
    kappa = np.exp(-1j * np.pi * fresnel_number * freq**2)
    prop = np.conj(dft) @ (kappa[:, None] * dft)
    tables = []
    for matrix in (prop, dft):
        re, im = matrix.real, matrix.imag
        right = np.block([[re, im], [-im, re]])
        left = np.block([[re, -im], [im, re]])
        tables.append(np.stack(split_table(right) + split_table(left)))
    return tables


def split(value):
    high = value.astype(BF16)
    low = (value - high.astype(F32)).astype(BF16)
    return high, low


def dot(a, b):
    return jnp.dot(a, b, preferred_element_type=F32)


def transform(re, im, tab):
    high, low = split(jnp.concatenate([re, im], axis=1))
    mid = dot(high, tab[0]) + dot(low, tab[0]) + dot(high, tab[1])
    mid = jnp.concatenate([mid[:, :LENGTH], mid[:, LENGTH:]], axis=0)
    high, low = split(mid)
    out = dot(tab[2], high) + dot(tab[2], low) + dot(tab[3], high)
    return out[:LENGTH], out[LENGTH:]


def cos_sin(angle):
    half = angle * 0.5
    sq = half * half
    s = -1.0 / 39916800.0
    for c in (1.0 / 362880.0, -1.0 / 5040.0, 1.0 / 120.0, -1.0 / 6.0, 1.0):
        s = s * sq + c
    s = s * half
    c = 1.0 / 479001600.0
    for k in (-1.0 / 3628800.0, 1.0 / 40320.0, -1.0 / 720.0, 1.0 / 24.0, -0.5, 1.0):
        c = c * sq + k
    return 1.0 - 2.0 * s * s, 2.0 * s * c


def masks(row, column):
    rows = lax.broadcasted_iota(jnp.int32, (LENGTH, LENGTH), 0)
    columns = lax.broadcasted_iota(jnp.int32, (LENGTH, LENGTH), 1)
    return rows >= row, columns >= column


def wrapped(own, below, in_strip, on_left):
    top = jnp.where(on_left, own[:, :LENGTH], own[:, LENGTH:])
    bottom = jnp.where(on_left, below[:, :LENGTH], below[:, LENGTH:])
    return jnp.where(in_strip, top, bottom)


def transmit(phase, absorb):
    magnitude = jnp.exp(-absorb)
    c, s = cos_sin(phase)
    return magnitude * c, magnitude * s


def roll2(value, row, column):
    return pltpu.roll(pltpu.roll(value, row, 0), column, 1)


def roll_kernel(offsets, probe, out):
    for slot in range(SLOTS):
        row, column = offsets[slot, 0], offsets[slot, 1] % LENGTH
        for mode in range(LOCAL_MODES):
            for part in range(2):
                out[slot, mode, part] = roll2(probe[mode, part], row, column)


def first_kernel(offsets, core, own_phase, own_absorb, halo_mine, halo_other, rolled, tab, wave, trans):
    swap = core[0] == 1
    below_phase = jnp.where(swap, halo_other[...], halo_mine[...])
    below_absorb = jnp.where(swap, halo_mine[...], halo_other[...])
    for slot in range(SLOTS):
        in_strip, on_left = masks(offsets[slot, 0], offsets[slot, 1])
        tr, ti = transmit(
            wrapped(own_phase[0], below_phase, in_strip, on_left),
            wrapped(own_absorb[0], below_absorb, in_strip, on_left),
        )
        trans[slot, 0] = tr
        trans[slot, 1] = ti
        for mode in range(LOCAL_MODES):
            pr, pi = rolled[slot, mode, 0], rolled[slot, mode, 1]
            wr, wi = transform(pr * tr - pi * ti, pr * ti + pi * tr, tab)
            wave[slot, mode, 0] = wr
            wave[slot, mode, 1] = wi


def second_kernel(slot, offsets, core, own_phase, own_absorb, halo_mine, halo_other, wave, tab, field, trans, keep, send, total):
    swap = core[0] == 1
    below_phase = jnp.where(swap, halo_other[...], halo_mine[...])
    below_absorb = jnp.where(swap, halo_mine[...], halo_other[...])
    in_strip, on_left = masks(offsets[slot, 0], offsets[slot, 1])
    tr, ti = transmit(
        wrapped(own_phase[0], below_phase, in_strip, on_left),
        wrapped(own_absorb[0], below_absorb, in_strip, on_left),
    )
    trans[0] = tr
    trans[1] = ti
    for mode in range(LOCAL_MODES):
        wr, wi = wave[0, mode, 0], wave[0, mode, 1]
        fr, fi = transform(wr * tr - wi * ti, wr * ti + wi * tr, tab)
        field[mode, 0] = fr
        field[mode, 1] = fi
        power = fr * fr + fi * fi
        total[...] = power if mode == 0 else total[...] + power
    low, high = total[:HALF], total[HALF:]
    keep[...] = jnp.where(swap, high, low)
    send[...] = jnp.where(swap, low, high)


def backward_kernel(
    slot, offsets, counts, core, mine, other, measured, field, wave, rolled, trans0, trans1, tab_a, tab_t,
    keep, send, grad_probe, factor,
):
    swap = core[0] == 1
    valid = (slot < counts[0]).astype(F32)
    low = jnp.where(swap, other[...], mine[...])
    high = jnp.where(swap, mine[...], other[...])
    intensity = jnp.concatenate([low, high], axis=0)
    factor[...] = valid * (1.0 - jnp.sqrt(measured[0] + 1.0) / jnp.sqrt(intensity + 1.0))

    def emit(layer, gr, gi, tr, ti):
        grads = (gi * tr - gr * ti, -(gr * tr + gi * ti))
        for kind in range(2):
            left, right = grads[kind][:, :HALF], grads[kind][:, HALF:]
            keep[layer, kind] = jnp.where(swap, right, left)
            send[layer, kind] = jnp.where(swap, left, right)

    row, column = offsets[slot, 0], offsets[slot, 1]
    back_row, back_column = (LENGTH - row) % LENGTH, (LENGTH - column) % LENGTH
    ur, ui = trans1[0], trans1[1]
    tr, ti = trans0[0, 0], trans0[0, 1]
    back = []
    sum_r = sum_i = None
    for mode in range(LOCAL_MODES):
        hr, hi = transform(factor[...] * field[mode, 0], -factor[...] * field[mode, 1], tab_t)
        wr, wi = wave[0, mode, 0], wave[0, mode, 1]
        gr = hr * wr - hi * wi
        gi = -(hr * wi + hi * wr)
        sum_r, sum_i = (gr, gi) if mode == 0 else (sum_r + gr, sum_i + gi)
        back.append((hr * ur - hi * ui, hr * ui + hi * ur))
    emit(1, sum_r, sum_i, ur, ui)
    for mode in range(LOCAL_MODES):
        hr, hi = transform(back[mode][0], back[mode][1], tab_a)
        pr, pi = rolled[0, mode, 0], rolled[0, mode, 1]
        gr = hr * pr - hi * pi
        gi = -(hr * pi + hi * pr)
        sum_r, sum_i = (gr, gi) if mode == 0 else (sum_r + gr, sum_i + gi)
        grad_probe[mode, 0] = roll2(hr * tr - hi * ti, back_row, back_column)
        grad_probe[mode, 1] = roll2(-(hr * ti + hi * tr), back_row, back_column)
    emit(0, sum_r, sum_i, tr, ti)


def fold_kernel(offsets, zhi, keep_a, keep_b, got_a, got_b, core, mine, send):
    rows = lax.broadcasted_iota(jnp.int32, (LENGTH, HALF), 0)
    columns = lax.broadcasted_iota(jnp.int32, (LENGTH, HALF), 1) + core[0] * HALF
    zero = jnp.zeros((LENGTH, HALF), F32)
    for layer in range(2):
        for kind in range(2):
            acc = None
            for slot, (keep, got) in enumerate(((keep_a, got_a), (keep_b, got_b))):
                value = keep[layer, kind] + got[layer, kind]
                in_strip = rows >= offsets[slot, 0]
                on_left = columns >= offsets[slot, 1]
                on_mine = jnp.logical_xor(on_left, zhi[0] == 1)
                pieces = [
                    jnp.where(jnp.logical_and(in_strip, on_mine), value, zero),
                    jnp.where(jnp.logical_or(in_strip, jnp.logical_not(on_mine)), zero, value),
                    jnp.where(jnp.logical_and(in_strip, jnp.logical_not(on_mine)), value, zero),
                    jnp.where(jnp.logical_or(in_strip, on_mine), zero, value),
                ]
                acc = pieces if acc is None else [a + b for a, b in zip(acc, pieces)]
            mine[0, layer, kind] = acc[0]
            mine[1, layer, kind] = acc[1]
            send[0, layer, kind] = acc[2]
            send[1, layer, kind] = acc[3]


VMEM = pl.BlockSpec(memory_space=pltpu.VMEM)
SMEM = pl.BlockSpec(memory_space=pltpu.SMEM)
PARAMS = pltpu.CompilerParams(vmem_limit_bytes=48 * 1024 * 1024)


def shape(*dims):
    return jax.ShapeDtypeStruct(dims, F32)


def whole(block, index):
    return pl.BlockSpec(block, lambda i: index)


def per_device(object_phase, object_absorb, probe_modes, measured, offsets, counts):
    layers, strip, columns = object_phase.shape
    mode_index = lax.axis_index("mode")
    core = (mode_index % 2).reshape(1)
    zhi = (mode_index // 2).reshape(1)
    up = [(i + 1, i) for i in range(TILES - 1)]
    down = [(i, i + 1) for i in range(TILES - 1)]
    cores = [(i, i ^ 1) for i in range(4)]
    far = [(i, i ^ 2) for i in range(4)]
    tab_a, tab_t = (jnp.asarray(t) for t in constant_tables())

    picked = jnp.where(core[0] == 0, object_phase, object_absorb)
    halo_mine = [lax.ppermute(picked[s], "tile", up) for s in range(layers)]
    rolled = pl.pallas_call(
        roll_kernel,
        out_shape=shape(SLOTS, LOCAL_MODES, 2, LENGTH, LENGTH),
        in_specs=[SMEM, VMEM],
        out_specs=VMEM,
        compiler_params=PARAMS,
    )(offsets, probe_modes)
    halo_other = [lax.ppermute(h, "mode", cores) for h in halo_mine]

    wave, trans0 = pl.pallas_call(
        first_kernel,
        grid=(1,),
        out_shape=(shape(SLOTS, LOCAL_MODES, 2, LENGTH, LENGTH), shape(SLOTS, 2, LENGTH, LENGTH)),
        in_specs=[
            SMEM,
            SMEM,
            whole((1, strip, columns), (0, 0, 0)),
            whole((1, strip, columns), (0, 0, 0)),
            VMEM,
            VMEM,
            VMEM,
            VMEM,
        ],
        out_specs=(VMEM, VMEM),
        compiler_params=PARAMS,
    )(offsets, core, object_phase, object_absorb, halo_mine[0], halo_other[0], rolled, tab_a)

    forward = []
    for slot in range(SLOTS):
        forward.append(
            pl.pallas_call(
                functools.partial(second_kernel, slot),
                grid=(1,),
                out_shape=(
                    shape(LOCAL_MODES, 2, LENGTH, LENGTH),
                    shape(2, LENGTH, LENGTH),
                    shape(HALF, LENGTH),
                    shape(HALF, LENGTH),
                ),
                in_specs=[
                    SMEM,
                    SMEM,
                    whole((1, strip, columns), (1, 0, 0)),
                    whole((1, strip, columns), (1, 0, 0)),
                    VMEM,
                    VMEM,
                    whole((1, LOCAL_MODES, 2, LENGTH, LENGTH), (slot, 0, 0, 0, 0)),
                    VMEM,
                ],
                out_specs=(VMEM,) * 4,
                scratch_shapes=[pltpu.VMEM((LENGTH, LENGTH), F32)],
                compiler_params=PARAMS,
            )(offsets, core, object_phase, object_absorb, halo_mine[1], halo_other[1], wave, tab_t)
        )

    back = []
    for slot in range(SLOTS):
        field, trans1, keep, send = forward[slot]
        pair = keep + lax.ppermute(send, "mode", cores)
        mine = pair + lax.ppermute(pair, "mode", far)
        other = lax.ppermute(mine, "mode", cores)
        back.append(
            pl.pallas_call(
                functools.partial(backward_kernel, slot),
                grid=(1,),
                out_shape=(
                    shape(2, 2, LENGTH, HALF),
                    shape(2, 2, LENGTH, HALF),
                    shape(LOCAL_MODES, 2, LENGTH, LENGTH),
                ),
                in_specs=[
                    SMEM,
                    SMEM,
                    SMEM,
                    VMEM,
                    VMEM,
                    whole((1, LENGTH, LENGTH), (slot, 0, 0)),
                    VMEM,
                    whole((1, LOCAL_MODES, 2, LENGTH, LENGTH), (slot, 0, 0, 0, 0)),
                    whole((1, LOCAL_MODES, 2, LENGTH, LENGTH), (slot, 0, 0, 0, 0)),
                    whole((1, 2, LENGTH, LENGTH), (slot, 0, 0, 0)),
                    VMEM,
                    VMEM,
                    VMEM,
                ],
                out_specs=(VMEM,) * 3,
                scratch_shapes=[pltpu.VMEM((LENGTH, LENGTH), F32)],
                compiler_params=PARAMS,
            )(offsets, counts, core, mine, other, measured, field, wave, rolled, trans0, trans1, tab_a, tab_t)
        )

    keep_a, send_a, probe_a = back[0]
    keep_b, send_b, probe_b = back[1]
    got_a = lax.ppermute(send_a, "mode", cores)
    got_b = lax.ppermute(send_b, "mode", cores)
    mine, send = pl.pallas_call(
        fold_kernel,
        out_shape=(shape(2, 2, 2, LENGTH, HALF), shape(2, 2, 2, LENGTH, HALF)),
        in_specs=[SMEM, SMEM, VMEM, VMEM, VMEM, VMEM, SMEM],
        out_specs=(VMEM, VMEM),
        compiler_params=PARAMS,
    )(offsets, zhi, keep_a, keep_b, got_a, got_b, core)
    got_next = lax.ppermute(send[1], "mode", far)
    got_own = lax.ppermute(send[0], "mode", far)
    from_above = lax.ppermute(mine[1] + got_next, "tile", down)

    grad_probe = (probe_a + probe_b).reshape(TILES, -1, LENGTH)
    share = jnp.sum(lax.all_to_all(grad_probe, "tile", 0, 0), axis=0)
    gathered = lax.all_to_all(jnp.broadcast_to(share[None], grad_probe.shape), "tile", 0, 0)
    probe_total = gathered.reshape(LOCAL_MODES, 2, LENGTH, LENGTH)

    grads = mine[0] + got_own + from_above
    return (grads[:, 0], grads[:, 1], probe_total)


def solution(mesh):
    in_specs = (
        P(None, "tile", None),
        P(None, "tile", None),
        P("mode", None, None, None),
        P("tile", None, None),
        P("tile", None),
        P("tile"),
    )
    out_specs = (P(None, "tile", "mode"), P(None, "tile", "mode"), P("mode", None, None, None))
    return jax.shard_map(
        per_device, mesh=mesh, in_specs=in_specs, out_specs=out_specs, check_vma=False
    )
```

```python
import functools
import math

import jax
import jax.numpy as jnp
import ml_dtypes
import numpy as np
from jax import lax
from jax.experimental import pallas as pl
from jax.experimental.pallas import tpu as pltpu
from jax.sharding import PartitionSpec as P

fresnel_number = 40.0
LENGTH = 256
HALF = LENGTH // 2
SLOTS = 2
LOCAL_MODES = 2
TILES = 32
F32 = jnp.float32
BF16 = jnp.bfloat16


def split_table(matrix):
    high = matrix.astype(ml_dtypes.bfloat16)
    low = (matrix - high.astype(np.float64)).astype(ml_dtypes.bfloat16)
    return high, low


@functools.lru_cache(maxsize=None)
def constant_tables():
    counter = np.arange(LENGTH)
    angle = 2.0 * np.pi / LENGTH * ((counter[:, None] * counter[None, :]) % LENGTH)
    dft = np.exp(-1j * angle) / math.sqrt(LENGTH)
    freq = ((counter + HALF) % LENGTH - HALF) / LENGTH
    kappa = np.exp(-1j * np.pi * fresnel_number * freq**2)
    prop = np.conj(dft) @ (kappa[:, None] * dft)
    tables = []
    for matrix in (prop, dft):
        highs, lows = zip(*(split_table(m) for m in (matrix.real, matrix.imag, matrix.real + matrix.imag)))
        tables.append(np.stack(highs + lows))
    return tables


def split(value):
    high = value.astype(BF16)
    low = (value - high.astype(F32)).astype(BF16)
    return high, low


def dot(a, b):
    return jnp.dot(a, b, preferred_element_type=F32)


def right_product(value, high, low):
    h, l = split(value)
    return dot(h, high) + dot(l, high) + dot(h, low)


def left_product(value, high, low):
    h, l = split(value)
    return dot(high, h) + dot(high, l) + dot(low, h)


def three_products(product, re, im, tab):
    a = product(re, tab[0], tab[3])
    b = product(im, tab[1], tab[4])
    c = product(re + im, tab[2], tab[5])
    return a - b, c - a - b


def transform(fields, tab):
    re, im = (jnp.concatenate([f[part] for f in fields], axis=0) for part in range(2))
    mid = three_products(right_product, re, im, tab)
    re, im = (
        jnp.concatenate([m[i * LENGTH : (i + 1) * LENGTH] for i in range(len(fields))], axis=1) for m in mid
    )
    re, im = three_products(left_product, re, im, tab)
    return [
        (re[:, i * LENGTH : (i + 1) * LENGTH], im[:, i * LENGTH : (i + 1) * LENGTH]) for i in range(len(fields))
    ]


def cos_sin(angle):
    half = angle * 0.5
    sq = half * half
    s = -1.0 / 39916800.0
    for c in (1.0 / 362880.0, -1.0 / 5040.0, 1.0 / 120.0, -1.0 / 6.0, 1.0):
        s = s * sq + c
    s = s * half
    c = 1.0 / 479001600.0
    for k in (-1.0 / 3628800.0, 1.0 / 40320.0, -1.0 / 720.0, 1.0 / 24.0, -0.5, 1.0):
        c = c * sq + k
    return 1.0 - 2.0 * s * s, 2.0 * s * c


def transmit(phase, absorb):
    magnitude = jnp.exp(-absorb)
    c, s = cos_sin(phase)
    return magnitude * c, magnitude * s


def roll2(value, row, column):
    return pltpu.roll(pltpu.roll(value, row, 0), column, 1)


def left_of(offsets, slot, shape):
    return lax.broadcasted_iota(jnp.int32, shape, 1) >= offsets[slot, 1]


def prepare_kernel(place, offsets, phase, absorb, probe, inside, rolled):
    on_left = left_of(offsets, place[0] // 2, PLANE)
    for layer in range(2):
        for kind, strip in enumerate((phase, absorb)):
            inside[layer, kind] = jnp.where(on_left, strip[layer, :, :LENGTH], strip[layer, :, LENGTH:])
    roll_probes(offsets, place, probe, rolled)


def pick_kernel(place, upper_offsets, phase, absorb, out):
    part = pl.ds(pl.multiple_of((place[0] % 2) * HALF, HALF), HALF)
    on_left = left_of(upper_offsets, place[0] // 2, (HALF, LENGTH))
    for layer in range(2):
        for kind, strip in enumerate((phase, absorb)):
            out[layer, kind] = jnp.where(on_left, strip[layer, part, :LENGTH], strip[layer, part, LENGTH:])


def slot_transmit(offsets, place, layer, inside, mine, other):
    swap = place[0] % 2 == 1
    in_strip = lax.broadcasted_iota(jnp.int32, PLANE, 0) >= offsets[place[0] // 2, 0]
    patch = []
    for kind in range(2):
        low = jnp.where(swap, other[layer, kind], mine[layer, kind])
        high = jnp.where(swap, mine[layer, kind], other[layer, kind])
        patch.append(jnp.where(in_strip, inside[layer, kind], jnp.concatenate([low, high], axis=0)))
    return transmit(*patch)


def roll_probes(offsets, place, probe, rolled):
    slot = place[0] // 2
    row, column = offsets[slot, 0], offsets[slot, 1] % LENGTH
    for m in range(probe.shape[0]):
        for part in range(2):
            rolled[m, part] = roll2(probe[m, part], row, column)


def through(fields, trans, tab):
    tr, ti = trans[0], trans[1]
    return transform([(f[0] * tr - f[1] * ti, f[0] * ti + f[1] * tr) for f in fields], tab)


def store(refs, fields):
    for m, (re, im) in enumerate(fields):
        refs[m, 0] = re
        refs[m, 1] = im


def forward_kernel(
    offsets, place, inside, mine, other, rolled_o, probe_f, tab_a, tab_t,
    rolled_f, wave_o, wave_f, field_o, field_f, trans0, trans1, power,
):
    trans0[0], trans0[1] = slot_transmit(offsets, place, 0, inside, mine, other)
    trans1[0], trans1[1] = slot_transmit(offsets, place, 1, inside, mine, other)
    roll_probes(offsets, place, probe_f, rolled_f)
    total = None
    for rolled, wave, field in ((rolled_o, wave_o, field_o), (rolled_f, wave_f, field_f)):
        store(wave, through([rolled[m] for m in range(LOCAL_MODES)], trans0, tab_a))
        fields = through([wave[m] for m in range(LOCAL_MODES)], trans1, tab_t)
        store(field, fields)
        term = sum(re * re + im * im for re, im in fields)
        total = term if total is None else total + term
    power[...] = total


def adjoint(offsets, place, factor, field, wave, rolled, trans0, trans1, tab_a, tab_t, put):
    slot = place[0] // 2
    row, column = offsets[slot, 0], offsets[slot, 1]
    back_row, back_column = (LENGTH - row) % LENGTH, (LENGTH - column) % LENGTH
    ur, ui = trans1[0], trans1[1]
    tr, ti = trans0[0], trans0[1]
    modes = range(LOCAL_MODES)
    back = transform([(factor * field[m, 0], -factor * field[m, 1]) for m in modes], tab_t)
    upper = (
        sum(hr * wave[m, 0] - hi * wave[m, 1] for m, (hr, hi) in enumerate(back)),
        -sum(hr * wave[m, 1] + hi * wave[m, 0] for m, (hr, hi) in enumerate(back)),
    )
    back = transform([(hr * ur - hi * ui, hr * ui + hi * ur) for hr, hi in back], tab_a)
    lower = (
        sum(hr * rolled[m, 0] - hi * rolled[m, 1] for m, (hr, hi) in enumerate(back)),
        -sum(hr * rolled[m, 1] + hi * rolled[m, 0] for m, (hr, hi) in enumerate(back)),
    )
    for m, (hr, hi) in enumerate(back):
        put(2 * m, roll2(hr * tr - hi * ti, back_row, back_column))
        put(2 * m + 1, roll2(-(hr * ti + hi * tr), back_row, back_column))
    return lower, upper


def backward_kernel(
    offsets, counts, place, power, near, measured, field_o, field_f, wave_o, wave_f, rolled_o, rolled_f,
    trans0, trans1, tab_a, tab_t, grads, keep, send, factor, partial, planes, sems,
):
    slot, swap = place[0] // 2, place[0] % 2 == 1
    valid = (slot < counts[0]).astype(F32)
    target = jnp.where(slot == 1, measured[1], measured[0])
    factor[...] = valid * (1.0 - jnp.sqrt(target + 1.0) / jnp.sqrt(power[...] + near[...] + 1.0))
    rest = (trans0, trans1, tab_a, tab_t)
    copies = []

    def put(index, value, foreign):
        planes[foreign, index] = value
        out = grads.at[jnp.bitwise_xor(slot, foreign), index]
        copies.append(pltpu.make_async_copy(planes.at[foreign, index], out, sems.at[foreign, index]))
        copies[-1].start()

    sums = adjoint(offsets, place, factor[...], field_f, wave_f, rolled_f, *rest, functools.partial(put, foreign=1))
    for layer in range(2):
        for part in range(2):
            partial[layer, part] = sums[layer][part]
    sums = adjoint(offsets, place, factor[...], field_o, wave_o, rolled_o, *rest, functools.partial(put, foreign=0))
    for layer, trans in enumerate((trans0, trans1)):
        gr, gi = (sums[layer][part] + partial[layer, part] for part in range(2))
        tr, ti = trans[0], trans[1]
        for kind, grad in enumerate((gi * tr - gr * ti, -(gr * tr + gi * ti))):
            left, right = grad[:, :HALF], grad[:, HALF:]
            keep[kind, layer] = jnp.where(swap, right, left)
            send[kind, layer] = jnp.where(swap, left, right)
    for copy in copies:
        copy.wait()


def fold_kernel(offsets, upper_offsets, place, pair, got, mine, send):
    core, zhi = place[0] % 2, place[0] // 2
    rows = lax.broadcasted_iota(jnp.int32, (LENGTH, HALF), 0)
    columns = lax.broadcasted_iota(jnp.int32, (LENGTH, HALF), 1) + core * HALF
    own_rows, upper_rows = rows >= offsets[zhi, 0], rows < upper_offsets[zhi, 0]
    own_mine = jnp.logical_xor(columns >= offsets[zhi, 1], zhi == 1)
    upper_mine = jnp.logical_xor(columns >= upper_offsets[zhi, 1], zhi == 1)
    for kind in range(2):
        for layer in range(2):
            own = jnp.where(own_rows, pair[kind, layer], 0.0)
            upper = jnp.where(upper_rows, got[kind, layer], 0.0)
            mine[kind, layer] = jnp.where(own_mine, own, 0.0) + jnp.where(upper_mine, upper, 0.0)
            send[kind, layer] = jnp.where(own_mine, 0.0, own) + jnp.where(upper_mine, 0.0, upper)


def sum_kernel(parts, after, out):
    del after
    total = parts[0]
    for i in range(1, parts.shape[0]):
        total += parts[i]
    out[...] = total


def spread_kernel(share, out):
    for i in range(out.shape[0]):
        out[i] = share[...]


VMEM = pl.BlockSpec(memory_space=pltpu.VMEM)
SMEM = pl.BlockSpec(memory_space=pltpu.SMEM)
ANY = pl.BlockSpec(memory_space=pl.ANY)
HBM = pl.BlockSpec(memory_space=pltpu.HBM)
PLANE = (LENGTH, LENGTH)
WAVE = (LOCAL_MODES, 2, LENGTH, LENGTH)
ONE = (1, 2, LENGTH, LENGTH)
PAIR = (2, LENGTH, LENGTH)
SHARE = (2, 2, LENGTH, HALF)
STRIPS = (2, 2, LENGTH, LENGTH)
HALVES = (2, 2, HALF, LENGTH)


def run(kernel, micros, scalars, outs, args, specs=None, scratch=(), out_specs=None, mib=24):
    return pl.pallas_call(
        kernel,
        out_shape=[jax.ShapeDtypeStruct(o, F32) for o in outs],
        in_specs=[SMEM] * scalars + (specs or [VMEM] * (len(args) - scalars)),
        out_specs=out_specs or [VMEM] * len(outs),
        scratch_shapes=scratch,
        compiler_params=pltpu.CompilerParams(vmem_limit_bytes=mib * 1024 * 1024),
        cost_estimate=pl.CostEstimate(flops=int(micros * 1.0e9), bytes_accessed=int(micros * 3.0e6), transcendentals=0),
    )(*args)


def per_device(object_phase, object_absorb, probe_modes, measured, offsets, counts):
    columns = object_phase.shape[2]
    place = lax.axis_index("mode").reshape(1)
    up = [(i + 1, i) for i in range(TILES - 1)]
    down = [(i, i + 1) for i in range(TILES - 1)]
    cores = [(i, i ^ 1) for i in range(4)]
    far = [(i, i ^ 2) for i in range(4)]
    flip = [(4 * t + m, 4 * (t ^ 4) + (m ^ 2)) for t in range(TILES) for m in range(4)]
    holders = [[4 * t + 2 * h + c for h in range(2) for t in range(TILES)] for c in range(2)]
    tab_a, tab_t = (jnp.asarray(t) for t in constant_tables())

    foreign = lax.ppermute(probe_modes, ("tile", "mode"), flip)
    upper_offsets = lax.ppermute(offsets, "tile", down)
    inside, rolled_o = run(
        prepare_kernel, 1.5, 2, [STRIPS, WAVE], (place, offsets, object_phase, object_absorb, probe_modes)
    )
    upper_offsets, inside = lax.optimization_barrier((upper_offsets, inside))
    (pick,) = run(pick_kernel, 0.5, 2, [HALVES], (place, upper_offsets, object_phase, object_absorb))
    mine = lax.ppermute(pick, "tile", up)
    other = lax.ppermute(mine, "mode", cores)
    rolled_f, wave_o, wave_f, field_o, field_f, trans0, trans1, power = run(
        forward_kernel,
        8.0,
        2,
        [WAVE] * 5 + [PAIR, PAIR, PLANE],
        (offsets, place, inside, mine, other, rolled_o, foreign, tab_a, tab_t),
    )
    near = lax.ppermute(power, "mode", cores)
    grads, keep, send = run(
        backward_kernel,
        9.0,
        3,
        [(2, 4) + PLANE, SHARE, SHARE],
        (
            offsets, counts, place, power, near, measured, field_o, field_f, wave_o, wave_f, rolled_o, rolled_f,
            trans0, trans1, tab_a, tab_t,
        ),
        scratch=[
            pltpu.VMEM(PLANE, F32),
            pltpu.VMEM((2, 2) + PLANE, F32),
            pltpu.VMEM((2, 4) + PLANE, F32),
            pltpu.SemaphoreType.DMA((2, 4)),
        ],
        out_specs=[HBM, VMEM, VMEM],
    )

    pair = keep + lax.ppermute(send, "mode", cores)
    got = lax.ppermute(pair, "tile", down)
    own, send = run(fold_kernel, 0.05, 3, [SHARE, SHARE], (offsets, upper_offsets, place, pair, got))
    from_far = lax.ppermute(send, "mode", far)
    grad_object = own + from_far

    grads = grads.reshape(2 * TILES, -1, LENGTH)
    parts = lax.all_to_all(grads, ("tile", "mode"), 0, 0, axis_index_groups=holders)
    (share,) = run(sum_kernel, 0.5, 0, [parts.shape[1:]], (parts, own), [VMEM, ANY])
    (spread,) = run(spread_kernel, 0.5, 0, [(TILES,) + share.shape], (share,))
    probe_total = lax.all_to_all(spread, "tile", 0, 0).reshape(WAVE)
    return (grad_object[0], grad_object[1], probe_total)


def solution(mesh):
    in_specs = (
        P(None, "tile", None),
        P(None, "tile", None),
        P("mode", None, None, None),
        P("tile", None, None),
        P("tile", None),
        P("tile"),
    )
    out_specs = (P(None, "tile", "mode"), P(None, "tile", "mode"), P("mode", None, None, None))
    return jax.shard_map(
        per_device, mesh=mesh, in_specs=in_specs, out_specs=out_specs, check_vma=False
    )
```

```python
import functools
import math

import jax
import jax.numpy as jnp
import ml_dtypes
import numpy as np
from jax import lax
from jax.experimental import pallas as pl
from jax.experimental.pallas import tpu as pltpu
from jax.sharding import PartitionSpec as P

fresnel_number = 40.0
LENGTH = 256
HALF = LENGTH // 2
SLOTS = 2
LOCAL_MODES = 2
TILES = 32
F32 = jnp.float32
BF16 = jnp.bfloat16


def split_table(matrix):
    high = matrix.astype(ml_dtypes.bfloat16)
    low = (matrix - high.astype(np.float64)).astype(ml_dtypes.bfloat16)
    return high, low


@functools.lru_cache(maxsize=None)
def constant_tables():
    counter = np.arange(LENGTH)
    angle = 2.0 * np.pi / LENGTH * ((counter[:, None] * counter[None, :]) % LENGTH)
    dft = np.exp(-1j * angle) / math.sqrt(LENGTH)
    freq = ((counter + HALF) % LENGTH - HALF) / LENGTH
    kappa = np.exp(-1j * np.pi * fresnel_number * freq**2)
    prop = np.conj(dft) @ (kappa[:, None] * dft)
    tables = []
    for matrix in (prop, dft):
        highs, lows = zip(*(split_table(m) for m in (matrix.real, matrix.imag, matrix.real + matrix.imag)))
        tables.append(np.stack(highs + lows))
    return tables


def split(value):
    high = value.astype(BF16)
    low = (value - high.astype(F32)).astype(BF16)
    return high, low


def dot(a, b):
    return jnp.dot(a, b, preferred_element_type=F32)


def right_product(value, high, low):
    h, l = split(value)
    return dot(h, high) + dot(l, high) + dot(h, low)


def left_product(value, high, low):
    h, l = split(value)
    return dot(high, h) + dot(high, l) + dot(low, h)


def three_products(product, re, im, tab):
    a = product(re, tab[0], tab[3])
    b = product(im, tab[1], tab[4])
    c = product(re + im, tab[2], tab[5])
    return a - b, c - a - b


def transform(fields, tab):
    re, im = (jnp.concatenate([f[part] for f in fields], axis=0) for part in range(2))
    mid = three_products(right_product, re, im, tab)
    re, im = (
        jnp.concatenate([m[i * LENGTH : (i + 1) * LENGTH] for i in range(len(fields))], axis=1) for m in mid
    )
    re, im = three_products(left_product, re, im, tab)
    return [
        (re[:, i * LENGTH : (i + 1) * LENGTH], im[:, i * LENGTH : (i + 1) * LENGTH]) for i in range(len(fields))
    ]


def cos_sin(angle):
    half = angle * 0.5
    sq = half * half
    s = -1.0 / 39916800.0
    for c in (1.0 / 362880.0, -1.0 / 5040.0, 1.0 / 120.0, -1.0 / 6.0, 1.0):
        s = s * sq + c
    s = s * half
    c = 1.0 / 479001600.0
    for k in (-1.0 / 3628800.0, 1.0 / 40320.0, -1.0 / 720.0, 1.0 / 24.0, -0.5, 1.0):
        c = c * sq + k
    return 1.0 - 2.0 * s * s, 2.0 * s * c


def transmit(phase, absorb):
    magnitude = jnp.exp(-absorb)
    c, s = cos_sin(phase)
    return magnitude * c, magnitude * s


def roll2(value, row, column):
    return pltpu.roll(pltpu.roll(value, row, 0), column, 1)


def left_of(offsets, slot, shape):
    return lax.broadcasted_iota(jnp.int32, shape, 1) >= offsets[slot, 1]


def roll_kernel(place, offsets, probe, rolled):
    roll_probes(offsets, place, probe, rolled)


def pick_kernel(place, upper_offsets, phase, absorb, out):
    part = pl.ds(pl.multiple_of((place[0] % 2) * HALF, HALF), HALF)
    on_left = left_of(upper_offsets, place[0] // 2, (HALF, LENGTH))
    for layer in range(2):
        for kind, strip in enumerate((phase, absorb)):
            out[layer, kind] = jnp.where(on_left, strip[layer, part, :LENGTH], strip[layer, part, LENGTH:])


def slot_transmit(offsets, place, layer, strips, mine, other):
    swap = place[0] % 2 == 1
    in_strip = lax.broadcasted_iota(jnp.int32, PLANE, 0) >= offsets[place[0] // 2, 0]
    on_left = left_of(offsets, place[0] // 2, PLANE)
    patch = []
    for kind in range(2):
        low = jnp.where(swap, other[layer, kind], mine[layer, kind])
        high = jnp.where(swap, mine[layer, kind], other[layer, kind])
        inside = jnp.where(on_left, strips[kind][layer, :, :LENGTH], strips[kind][layer, :, LENGTH:])
        patch.append(jnp.where(in_strip, inside, jnp.concatenate([low, high], axis=0)))
    return transmit(*patch)


def roll_probes(offsets, place, probe, rolled):
    slot = place[0] // 2
    row, column = offsets[slot, 0], offsets[slot, 1] % LENGTH
    for m in range(probe.shape[0]):
        for part in range(2):
            rolled[m, part] = roll2(probe[m, part], row, column)


def through(fields, trans, tab):
    tr, ti = trans[0], trans[1]
    return transform([(f[0] * tr - f[1] * ti, f[0] * ti + f[1] * tr) for f in fields], tab)


def store(refs, fields):
    for m, (re, im) in enumerate(fields):
        refs[m, 0] = re
        refs[m, 1] = im


def forward_kernel(
    offsets, place, phase, absorb, mine, other, rolled_o, probe_f, tab_a, tab_t,
    rolled_f, wave_o, wave_f, field_o, field_f, trans0, trans1, power,
):
    trans0[0], trans0[1] = slot_transmit(offsets, place, 0, (phase, absorb), mine, other)
    trans1[0], trans1[1] = slot_transmit(offsets, place, 1, (phase, absorb), mine, other)
    roll_probes(offsets, place, probe_f, rolled_f)
    total = None
    for rolled, wave, field in ((rolled_o, wave_o, field_o), (rolled_f, wave_f, field_f)):
        store(wave, through([rolled[m] for m in range(LOCAL_MODES)], trans0, tab_a))
        fields = through([wave[m] for m in range(LOCAL_MODES)], trans1, tab_t)
        store(field, fields)
        term = sum(re * re + im * im for re, im in fields)
        total = term if total is None else total + term
    power[...] = total


def adjoint(offsets, place, factor, field, wave, rolled, trans0, trans1, tab_a, tab_t, grads, which):
    slot = place[0] // 2
    row, column = offsets[slot, 0], offsets[slot, 1]
    back_row, back_column = (LENGTH - row) % LENGTH, (LENGTH - column) % LENGTH
    ur, ui = trans1[0], trans1[1]
    tr, ti = trans0[0], trans0[1]
    modes = range(LOCAL_MODES)
    back = transform([(factor * field[m, 0], -factor * field[m, 1]) for m in modes], tab_t)
    upper = (
        sum(hr * wave[m, 0] - hi * wave[m, 1] for m, (hr, hi) in enumerate(back)),
        -sum(hr * wave[m, 1] + hi * wave[m, 0] for m, (hr, hi) in enumerate(back)),
    )
    back = transform([(hr * ur - hi * ui, hr * ui + hi * ur) for hr, hi in back], tab_a)
    lower = (
        sum(hr * rolled[m, 0] - hi * rolled[m, 1] for m, (hr, hi) in enumerate(back)),
        -sum(hr * rolled[m, 1] + hi * rolled[m, 0] for m, (hr, hi) in enumerate(back)),
    )
    for m, (hr, hi) in enumerate(back):
        for part, value in enumerate((hr * tr - hi * ti, -(hr * ti + hi * tr))):
            value = roll2(value, back_row, back_column)
            for i in range(4):
                grads[4 * (2 * m + part) + i, which] = value[i * CHUNK : (i + 1) * CHUNK]
    return lower, upper


def backward_kernel(
    offsets, counts, place, power, near, measured, field_o, field_f, wave_o, wave_f, rolled_o, rolled_f,
    trans0, trans1, tab_a, tab_t, grads, keep, send, factor, partial,
):
    slot, swap = place[0] // 2, place[0] % 2 == 1
    valid = (slot < counts[0]).astype(F32)
    target = jnp.where(slot == 1, measured[1], measured[0])
    factor[...] = valid * (1.0 - jnp.sqrt(target + 1.0) / jnp.sqrt(power[...] + near[...] + 1.0))
    rest = (trans0, trans1, tab_a, tab_t)
    sums = adjoint(offsets, place, factor[...], field_f, wave_f, rolled_f, *rest, grads, 1)
    for layer in range(2):
        for part in range(2):
            partial[layer, part] = sums[layer][part]
    sums = adjoint(offsets, place, factor[...], field_o, wave_o, rolled_o, *rest, grads, 0)
    for layer, trans in enumerate((trans0, trans1)):
        gr, gi = (sums[layer][part] + partial[layer, part] for part in range(2))
        tr, ti = trans[0], trans[1]
        for kind, grad in enumerate((gi * tr - gr * ti, -(gr * tr + gi * ti))):
            left, right = grad[:, :HALF], grad[:, HALF:]
            keep[kind, layer] = jnp.where(swap, right, left)
            send[kind, layer] = jnp.where(swap, left, right)


def fold_kernel(offsets, place, pair, far_pair, own, below):
    core, zhi = place[0] % 2, place[0] // 2
    rows = lax.broadcasted_iota(jnp.int32, (LENGTH, HALF), 0)
    columns = lax.broadcasted_iota(jnp.int32, (LENGTH, HALF), 1) + core * HALF
    where = []
    for slot in (zhi, 1 - zhi):
        on_mine = jnp.logical_xor(columns >= offsets[slot, 1], zhi == 1)
        where.append((on_mine, rows >= offsets[slot, 0]))
    for kind in range(2):
        for layer in range(2):
            sums = [0.0, 0.0]
            for (on_mine, in_strip), source in zip(where, (pair, far_pair)):
                value = jnp.where(on_mine, source[kind, layer], 0.0)
                inside = jnp.where(in_strip, value, 0.0)
                sums = [sums[0] + inside, sums[1] + (value - inside)]
            own[kind, layer], below[kind, layer] = sums


def sum_kernel(parts, after, own, foreign):
    del after
    for which, out in enumerate((own, foreign)):
        total = parts[0, which]
        for i in range(1, parts.shape[0]):
            total += parts[i, which]
        out[...] = total


def spread_kernel(share, far, after, out):
    del after
    total = share[...] + far[...]
    for i in range(out.shape[0]):
        out[i] = total


VMEM = pl.BlockSpec(memory_space=pltpu.VMEM)
SMEM = pl.BlockSpec(memory_space=pltpu.SMEM)
ANY = pl.BlockSpec(memory_space=pl.ANY)
HBM = pl.BlockSpec(memory_space=pltpu.HBM)
PLANE = (LENGTH, LENGTH)
CHUNKS, CHUNK = 16, 64
WAVE = (LOCAL_MODES, 2, LENGTH, LENGTH)
ONE = (1, 2, LENGTH, LENGTH)
PAIR = (2, LENGTH, LENGTH)
SHARE = (2, 2, LENGTH, HALF)
HALVES = (2, 2, HALF, LENGTH)


def run(kernel, micros, scalars, outs, args, specs=None, scratch=(), out_specs=None, mib=24):
    return pl.pallas_call(
        kernel,
        out_shape=[jax.ShapeDtypeStruct(o, F32) for o in outs],
        in_specs=[SMEM] * scalars + (specs or [VMEM] * (len(args) - scalars)),
        out_specs=out_specs or [VMEM] * len(outs),
        scratch_shapes=scratch,
        compiler_params=pltpu.CompilerParams(vmem_limit_bytes=mib * 1024 * 1024),
        cost_estimate=pl.CostEstimate(flops=int(micros * 1.0e9), bytes_accessed=int(micros * 3.0e6), transcendentals=0),
    )(*args)


def per_device(object_phase, object_absorb, probe_modes, measured, offsets, counts):
    columns = object_phase.shape[2]
    place = lax.axis_index("mode").reshape(1)
    up = [(i + 1, i) for i in range(TILES - 1)]
    down = [(i, i + 1) for i in range(TILES - 1)]
    cores = [(i, i ^ 1) for i in range(4)]
    far = [(i, i ^ 2) for i in range(4)]
    flip = [(4 * t + m, 4 * (t ^ 4) + (m ^ 2)) for t in range(TILES) for m in range(4)]
    planes = [[(x * 2 + z) * 4 + y for x in range(4) for y in range(4)] for z in range(2)]
    across = [(i, i ^ 4) for i in range(TILES)]
    tab_a, tab_t = (jnp.asarray(t) for t in constant_tables())

    foreign = lax.ppermute(probe_modes, ("tile", "mode"), flip)
    upper_offsets = lax.ppermute(offsets, "tile", down)
    (rolled_o,) = run(roll_kernel, 0.05, 2, [WAVE], (place, offsets, probe_modes))
    (pick,) = run(pick_kernel, 0.5, 2, [HALVES], (place, upper_offsets, object_phase, object_absorb))
    mine = lax.ppermute(pick, "tile", up)
    other = lax.ppermute(mine, "mode", cores)
    rolled_f, wave_o, wave_f, field_o, field_f, trans0, trans1, power = run(
        forward_kernel,
        8.0,
        2,
        [WAVE] * 5 + [PAIR, PAIR, PLANE],
        (offsets, place, object_phase, object_absorb, mine, other, rolled_o, foreign, tab_a, tab_t),
    )
    near = lax.ppermute(power, "mode", cores)
    grads, keep, send = run(
        backward_kernel,
        9.0,
        3,
        [(CHUNKS, 2, CHUNK, LENGTH), SHARE, SHARE],
        (
            offsets, counts, place, power, near, measured, field_o, field_f, wave_o, wave_f, rolled_o, rolled_f,
            trans0, trans1, tab_a, tab_t,
        ),
        scratch=[pltpu.VMEM(PLANE, F32), pltpu.VMEM((2, 2) + PLANE, F32)],
    )

    pair = keep + lax.ppermute(send, "mode", cores)
    far_pair = lax.ppermute(pair, "mode", far)
    own, below = run(fold_kernel, 0.05, 2, [SHARE, SHARE], (offsets, place, pair, far_pair))
    above = lax.ppermute(below, "tile", down)
    grad_object = own + above

    parts = lax.all_to_all(grads, "tile", 0, 0, axis_index_groups=planes)
    share, share_f = run(sum_kernel, 0.5, 0, [(CHUNK, LENGTH)] * 2, (parts, below), [VMEM, ANY])
    share += lax.ppermute(share_f, ("tile", "mode"), flip)
    far_share = lax.ppermute(share, "tile", across)
    (spread,) = run(spread_kernel, 0.5, 0, [(CHUNKS, CHUNK, LENGTH)], (share, far_share, above), [VMEM, VMEM, ANY])
    probe_total = lax.all_to_all(spread, "tile", 0, 0, axis_index_groups=planes).reshape(WAVE)
    return (grad_object[0], grad_object[1], probe_total)


def solution(mesh):
    in_specs = (
        P(None, "tile", None),
        P(None, "tile", None),
        P("mode", None, None, None),
        P("tile", None, None),
        P("tile", None),
        P("tile"),
    )
    out_specs = (P(None, "tile", "mode"), P(None, "tile", "mode"), P("mode", None, None, None))
    return jax.shard_map(
        per_device, mesh=mesh, in_specs=in_specs, out_specs=out_specs, check_vma=False
    )
```

```python
import functools
import math

import jax
import jax.numpy as jnp
import ml_dtypes
import numpy as np
from jax import lax
from jax.experimental import pallas as pl
from jax.experimental.pallas import tpu as pltpu
from jax.sharding import PartitionSpec as P

fresnel_number = 40.0
LENGTH = 256
HALF = LENGTH // 2
SLOTS = 2
LOCAL_MODES = 2
TILES = 32
F32 = jnp.float32
BF16 = jnp.bfloat16


def split_table(matrix):
    high = matrix.astype(ml_dtypes.bfloat16)
    low = (matrix - high.astype(np.float64)).astype(ml_dtypes.bfloat16)
    return high, low


@functools.lru_cache(maxsize=None)
def constant_tables():
    counter = np.arange(LENGTH)
    angle = 2.0 * np.pi / LENGTH * ((counter[:, None] * counter[None, :]) % LENGTH)
    dft = np.exp(-1j * angle) / math.sqrt(LENGTH)
    freq = ((counter + HALF) % LENGTH - HALF) / LENGTH
    kappa = np.exp(-1j * np.pi * fresnel_number * freq**2)
    prop = np.conj(dft) @ (kappa[:, None] * dft)
    tables = []
    for matrix in (prop, dft):
        highs, lows = zip(*(split_table(m) for m in (matrix.real, matrix.imag, matrix.real + matrix.imag)))
        tables.append(np.stack(highs + lows))
    return tables


def split(value):
    high = value.astype(BF16)
    low = (value - high.astype(F32)).astype(BF16)
    return high, low


def dot(a, b):
    return jnp.dot(a, b, preferred_element_type=F32)


def right_product(value, high, low):
    h, l = split(value)
    return dot(h, high) + dot(l, high) + dot(h, low)


def left_product(value, high, low):
    h, l = split(value)
    return dot(high, h) + dot(high, l) + dot(low, h)


def three_products(product, re, im, tab):
    a = product(re, tab[0], tab[3])
    b = product(im, tab[1], tab[4])
    c = product(re + im, tab[2], tab[5])
    return a - b, c - a - b


def transform(fields, tab):
    re, im = (jnp.concatenate([f[part] for f in fields], axis=0) for part in range(2))
    mid = three_products(right_product, re, im, tab)
    re, im = (
        jnp.concatenate([m[i * LENGTH : (i + 1) * LENGTH] for i in range(len(fields))], axis=1) for m in mid
    )
    re, im = three_products(left_product, re, im, tab)
    return [
        (re[:, i * LENGTH : (i + 1) * LENGTH], im[:, i * LENGTH : (i + 1) * LENGTH]) for i in range(len(fields))
    ]


def cos_sin(angle):
    half = angle * 0.5
    sq = half * half
    s = -1.0 / 39916800.0
    for c in (1.0 / 362880.0, -1.0 / 5040.0, 1.0 / 120.0, -1.0 / 6.0, 1.0):
        s = s * sq + c
    s = s * half
    c = 1.0 / 479001600.0
    for k in (-1.0 / 3628800.0, 1.0 / 40320.0, -1.0 / 720.0, 1.0 / 24.0, -0.5, 1.0):
        c = c * sq + k
    return 1.0 - 2.0 * s * s, 2.0 * s * c


def transmit(phase, absorb):
    magnitude = jnp.exp(-absorb)
    c, s = cos_sin(phase)
    return magnitude * c, magnitude * s


def roll2(value, row, column):
    return pltpu.roll(pltpu.roll(value, row, 0), column, 1)


def left_of(offsets, slot, shape):
    return lax.broadcasted_iota(jnp.int32, shape, 1) >= offsets[slot, 1]


def roll_kernel(place, offsets, probe, rolled):
    roll_probes(offsets, place, probe, rolled)


def pick_kernel(place, upper_offsets, phase, absorb, out):
    part = pl.ds(pl.multiple_of((place[0] % 2) * HALF, HALF), HALF)
    on_left = left_of(upper_offsets, place[0] // 2, (HALF, LENGTH))
    for layer in range(2):
        for kind, strip in enumerate((phase, absorb)):
            out[layer, kind] = jnp.where(on_left, strip[layer, part, :LENGTH], strip[layer, part, LENGTH:])


def slot_transmit(offsets, place, layer, strips, mine, other):
    swap = place[0] % 2 == 1
    in_strip = lax.broadcasted_iota(jnp.int32, PLANE, 0) >= offsets[place[0] // 2, 0]
    on_left = left_of(offsets, place[0] // 2, PLANE)
    patch = []
    for kind in range(2):
        low = jnp.where(swap, other[layer, kind], mine[layer, kind])
        high = jnp.where(swap, mine[layer, kind], other[layer, kind])
        inside = jnp.where(on_left, strips[kind][layer, :, :LENGTH], strips[kind][layer, :, LENGTH:])
        patch.append(jnp.where(in_strip, inside, jnp.concatenate([low, high], axis=0)))
    return transmit(*patch)


def roll_probes(offsets, place, probe, rolled):
    slot = place[0] // 2
    row, column = offsets[slot, 0], offsets[slot, 1] % LENGTH
    for m in range(probe.shape[0]):
        for part in range(2):
            rolled[m, part] = roll2(probe[m, part], row, column)


def through(fields, trans, tab):
    tr, ti = trans[0], trans[1]
    return transform([(f[0] * tr - f[1] * ti, f[0] * ti + f[1] * tr) for f in fields], tab)


def store(refs, fields):
    for m, (re, im) in enumerate(fields):
        refs[m, 0] = re
        refs[m, 1] = im


def forward_kernel(
    offsets, place, phase, absorb, mine, other, rolled_o, probe_f, tab_a, tab_t,
    rolled_f, wave_o, wave_f, field_o, field_f, trans0, trans1, power,
):
    trans0[0], trans0[1] = slot_transmit(offsets, place, 0, (phase, absorb), mine, other)
    trans1[0], trans1[1] = slot_transmit(offsets, place, 1, (phase, absorb), mine, other)
    roll_probes(offsets, place, probe_f, rolled_f)
    total = None
    for rolled, wave, field in ((rolled_o, wave_o, field_o), (rolled_f, wave_f, field_f)):
        store(wave, through([rolled[m] for m in range(LOCAL_MODES)], trans0, tab_a))
        fields = through([wave[m] for m in range(LOCAL_MODES)], trans1, tab_t)
        store(field, fields)
        term = sum(re * re + im * im for re, im in fields)
        total = term if total is None else total + term
    power[...] = total


def adjoint(offsets, place, factor, field, wave, rolled, trans0, trans1, tab_a, tab_t, grads, which):
    slot = place[0] // 2
    row, column = offsets[slot, 0], offsets[slot, 1]
    back_row, back_column = (LENGTH - row) % LENGTH, (LENGTH - column) % LENGTH
    ur, ui = trans1[0], trans1[1]
    tr, ti = trans0[0], trans0[1]
    modes = range(LOCAL_MODES)
    back = transform([(factor * field[m, 0], -factor * field[m, 1]) for m in modes], tab_t)
    upper = (
        sum(hr * wave[m, 0] - hi * wave[m, 1] for m, (hr, hi) in enumerate(back)),
        -sum(hr * wave[m, 1] + hi * wave[m, 0] for m, (hr, hi) in enumerate(back)),
    )
    back = transform([(hr * ur - hi * ui, hr * ui + hi * ur) for hr, hi in back], tab_a)
    lower = (
        sum(hr * rolled[m, 0] - hi * rolled[m, 1] for m, (hr, hi) in enumerate(back)),
        -sum(hr * rolled[m, 1] + hi * rolled[m, 0] for m, (hr, hi) in enumerate(back)),
    )
    for m, (hr, hi) in enumerate(back):
        for part, value in enumerate((hr * tr - hi * ti, -(hr * ti + hi * tr))):
            value = roll2(value, back_row, back_column)
            for i in range(4):
                grads[4 * (2 * m + part) + i, which] = value[i * CHUNK : (i + 1) * CHUNK]
    return lower, upper


def backward_kernel(
    offsets, counts, place, power, near, measured, field_o, field_f, wave_o, wave_f, rolled_o, rolled_f,
    trans0, trans1, tab_a, tab_t, grads, keep, send, factor, partial,
):
    slot, swap = place[0] // 2, place[0] % 2 == 1
    valid = (slot < counts[0]).astype(F32)
    target = jnp.where(slot == 1, measured[1], measured[0])
    factor[...] = valid * (1.0 - jnp.sqrt(target + 1.0) / jnp.sqrt(power[...] + near[...] + 1.0))
    rest = (trans0, trans1, tab_a, tab_t)
    sums = adjoint(offsets, place, factor[...], field_f, wave_f, rolled_f, *rest, grads, 1)
    for layer in range(2):
        for part in range(2):
            partial[layer, part] = sums[layer][part]
    sums = adjoint(offsets, place, factor[...], field_o, wave_o, rolled_o, *rest, grads, 0)
    for layer, trans in enumerate((trans0, trans1)):
        gr, gi = (sums[layer][part] + partial[layer, part] for part in range(2))
        tr, ti = trans[0], trans[1]
        for kind, grad in enumerate((gi * tr - gr * ti, -(gr * tr + gi * ti))):
            left, right = grad[:, :HALF], grad[:, HALF:]
            keep[kind, layer] = jnp.where(swap, right, left)
            send[kind, layer] = jnp.where(swap, left, right)


def fold_kernel(offsets, upper_offsets, place, pair, got, mine, send):
    core, zhi = place[0] % 2, place[0] // 2
    rows = lax.broadcasted_iota(jnp.int32, (LENGTH, HALF), 0)
    columns = lax.broadcasted_iota(jnp.int32, (LENGTH, HALF), 1) + core * HALF
    own_rows, upper_rows = rows >= offsets[zhi, 0], rows < upper_offsets[zhi, 0]
    own_mine = jnp.logical_xor(columns >= offsets[zhi, 1], zhi == 1)
    upper_mine = jnp.logical_xor(columns >= upper_offsets[zhi, 1], zhi == 1)
    for kind in range(2):
        for layer in range(2):
            own = jnp.where(own_rows, pair[kind, layer], 0.0)
            upper = jnp.where(upper_rows, got[kind, layer], 0.0)
            mine[kind, layer] = jnp.where(own_mine, own, 0.0) + jnp.where(upper_mine, upper, 0.0)
            send[kind, layer] = jnp.where(own_mine, 0.0, own) + jnp.where(upper_mine, 0.0, upper)


def sum_kernel(parts, own, foreign):
    for which, out in enumerate((own, foreign)):
        total = parts[0, which]
        for i in range(1, parts.shape[0]):
            total += parts[i, which]
        out[...] = total


def spread_kernel(share, far, out):
    total = share[...] + far[...]
    for i in range(out.shape[0]):
        out[i] = total


VMEM = pl.BlockSpec(memory_space=pltpu.VMEM)
SMEM = pl.BlockSpec(memory_space=pltpu.SMEM)
ANY = pl.BlockSpec(memory_space=pl.ANY)
HBM = pl.BlockSpec(memory_space=pltpu.HBM)
PLANE = (LENGTH, LENGTH)
CHUNKS, CHUNK = 16, 64
WAVE = (LOCAL_MODES, 2, LENGTH, LENGTH)
ONE = (1, 2, LENGTH, LENGTH)
PAIR = (2, LENGTH, LENGTH)
SHARE = (2, 2, LENGTH, HALF)
HALVES = (2, 2, HALF, LENGTH)


def run(kernel, micros, scalars, outs, args, specs=None, scratch=(), out_specs=None, mib=24):
    return pl.pallas_call(
        kernel,
        out_shape=[jax.ShapeDtypeStruct(o, F32) for o in outs],
        in_specs=[SMEM] * scalars + (specs or [VMEM] * (len(args) - scalars)),
        out_specs=out_specs or [VMEM] * len(outs),
        scratch_shapes=scratch,
        compiler_params=pltpu.CompilerParams(vmem_limit_bytes=mib * 1024 * 1024),
        cost_estimate=pl.CostEstimate(flops=int(micros * 1.0e9), bytes_accessed=int(micros * 3.0e6), transcendentals=0),
    )(*args)


def per_device(object_phase, object_absorb, probe_modes, measured, offsets, counts):
    columns = object_phase.shape[2]
    place = lax.axis_index("mode").reshape(1)
    up = [(i + 1, i) for i in range(TILES - 1)]
    down = [(i, i + 1) for i in range(TILES - 1)]
    cores = [(i, i ^ 1) for i in range(4)]
    far = [(i, i ^ 2) for i in range(4)]
    flip = [(4 * t + m, 4 * (t ^ 4) + (m ^ 2)) for t in range(TILES) for m in range(4)]
    planes = [[(x * 2 + z) * 4 + y for x in range(4) for y in range(4)] for z in range(2)]
    across = [(i, i ^ 4) for i in range(TILES)]
    tab_a, tab_t = (jnp.asarray(t) for t in constant_tables())

    foreign = lax.ppermute(probe_modes, ("tile", "mode"), flip)
    upper_offsets = lax.ppermute(offsets, "tile", down)
    (rolled_o,) = run(roll_kernel, 0.05, 2, [WAVE], (place, offsets, probe_modes))
    (pick,) = run(pick_kernel, 0.5, 2, [HALVES], (place, upper_offsets, object_phase, object_absorb))
    mine = lax.ppermute(pick, "tile", up)
    other = lax.ppermute(mine, "mode", cores)
    rolled_f, wave_o, wave_f, field_o, field_f, trans0, trans1, power = run(
        forward_kernel,
        8.0,
        2,
        [WAVE] * 5 + [PAIR, PAIR, PLANE],
        (offsets, place, object_phase, object_absorb, mine, other, rolled_o, foreign, tab_a, tab_t),
    )
    near = lax.ppermute(power, "mode", cores)
    grads, keep, send = run(
        backward_kernel,
        9.0,
        3,
        [(CHUNKS, 2, CHUNK, LENGTH), SHARE, SHARE],
        (
            offsets, counts, place, power, near, measured, field_o, field_f, wave_o, wave_f, rolled_o, rolled_f,
            trans0, trans1, tab_a, tab_t,
        ),
        scratch=[pltpu.VMEM(PLANE, F32), pltpu.VMEM((2, 2) + PLANE, F32)],
    )

    pair = keep + lax.ppermute(send, "mode", cores)
    got = lax.ppermute(pair, "tile", down)
    own, send = run(fold_kernel, 0.05, 3, [SHARE, SHARE], (offsets, upper_offsets, place, pair, got))
    from_far = lax.ppermute(send, "mode", far)
    grad_object = own + from_far

    parts = lax.all_to_all(grads, "tile", 0, 0, axis_index_groups=planes)
    share, share_f = run(sum_kernel, 0.5, 0, [(CHUNK, LENGTH)] * 2, (parts,))
    share += lax.ppermute(share_f, ("tile", "mode"), flip)
    far_share = lax.ppermute(share, "tile", across)
    (spread,) = run(spread_kernel, 0.5, 0, [(CHUNKS, CHUNK, LENGTH)], (share, far_share))
    probe_total = lax.all_to_all(spread, "tile", 0, 0, axis_index_groups=planes).reshape(WAVE)
    return (grad_object[0], grad_object[1], probe_total)


def solution(mesh):
    in_specs = (
        P(None, "tile", None),
        P(None, "tile", None),
        P("mode", None, None, None),
        P("tile", None, None),
        P("tile", None),
        P("tile"),
    )
    out_specs = (P(None, "tile", "mode"), P(None, "tile", "mode"), P("mode", None, None, None))
    return jax.shard_map(
        per_device, mesh=mesh, in_specs=in_specs, out_specs=out_specs, check_vma=False
    )
```
